32 devices in a mesh: grp: 4 (over x, core), mz: 8 (over z, y).
Axes of the slice: x: 2, y: 2, z: 4, core: 2. Of those that a mesh axis runs over, the one named last changes fastest.
Arguments:
- intensities: float32 [512, 8, 32768], P('grp', None, 'mz'), as said below
- sample_start: float32 [512, 256], P('grp'), as said below
- scan_start: float32 [8, 256], replicated, as said below
- mass_start: float32 [32768, 256], P('mz'), as said below
Outputs:
- sample_factor: float32 [512, 256], P('grp')
- scan_factor: float32 [8, 256], replicated
- mass_factor: float32 [32768, 256], P('mz')
Inputs may be any that keep to these rules, and one draw needn't show every extreme that they name: Measured intensities of the cohort. `sample_start`: a starting estimate of the sample factor. `scan_start`: a starting estimate of the scan factor. `mass_start`: a starting estimate of the m/z factor.
All inputs are finite; a program needn't handle non-finite values.
Results may differ from the reference program's by a relative error of at most 0.0001.
Values sent between devices are 32-bit elements; how exact they have to be, the bound alone decides.
No kernel may reach another device: no remote copies, remote signals or barrier semaphores. Data moves between devices by JAX's collectives and lax.ppermute only.
A program may use at most 128 MiB of HBM per device.

```python
import math
import jax
import jax.numpy as jnp
from jax import lax

RANK = 256
SCANS = 8
STEPS = 2
SAMPLES = 512
BINS = 32768


def truth_factor(key, height, code, rising):
    first, second = jax.random.split(jax.random.fold_in(key, code), 2)
    random_part = jax.random.normal(first, (height, RANK), jnp.float32)
    shared = jax.random.normal(second, (height, 1), jnp.float32)
    slope = 2.0
    factor = random_part + shared
    if rising:
        position = jnp.arange(height, dtype=jnp.float32) / (height - 1.0)
        factor = factor * jnp.sqrt(1.0 + slope * position)[:, None]
    return factor


def perturbed(key, truth, code):
    noise_key = jax.random.fold_in(key, code)
    noise = 0.25 * jax.random.normal(noise_key, truth.shape, jnp.float32)
    return truth * (1.0 + noise)


def draw_intensities(key, part):
    sample_true = truth_factor(key, SAMPLES, 11, True)
    scan_true = truth_factor(key, SCANS, 23, False)
    mass_true = truth_factor(key, BINS, 37, True)
    khatri = (sample_true[:, None, :] * scan_true[None, :, :]).reshape(SAMPLES * SCANS, RANK)
    planted = jnp.dot(khatri, mass_true.T, precision=lax.Precision.HIGHEST, preferred_element_type=jnp.float32)
    noise = jax.random.normal(jax.random.fold_in(key, 53), (SAMPLES * SCANS, BINS), jnp.float32) * math.sqrt(RANK)
    return (planted + noise).reshape(SAMPLES, SCANS, BINS)


def draw_sample_start(key, part):
    return perturbed(key, truth_factor(key, SAMPLES, 11, True), 61)


def draw_scan_start(key, part):
    return perturbed(key, truth_factor(key, SCANS, 23, False), 67)


def draw_mass_start(key, part):
    return perturbed(key, truth_factor(key, BINS, 37, True), 71)


def setup_inputs(seed: int = 0) -> dict:
    key_list = jax.random.split(jax.random.key(seed), 5)
    intensities = draw_intensities(jax.random.fold_in(key_list[4], 71), 0)
    sample_start = draw_sample_start(jax.random.fold_in(key_list[4], 71), 0)
    scan_start = draw_scan_start(jax.random.fold_in(key_list[4], 71), 0)
    mass_start = draw_mass_start(jax.random.fold_in(key_list[4], 71), 0)
    return dict(intensities=intensities, sample_start=sample_start, scan_start=scan_start, mass_start=mass_start)


precise = lax.Precision.HIGHEST

def frobenius(gram):
    return jnp.sqrt(jnp.sum(gram * gram) + 1e-12)

def reference(intensities, sample_start, scan_start, mass_start):
    factor_a = sample_start
    factor_b = scan_start
    factor_c = mass_start
    unfolded = intensities.reshape(SAMPLES * SCANS, BINS)
    for iteration in range(STEPS):
        gram_a = jnp.dot(factor_a.T, factor_a, precision=precise, preferred_element_type=jnp.float32)
        gram_b = jnp.dot(factor_b.T, factor_b, precision=precise, preferred_element_type=jnp.float32)
        gram_c = jnp.dot(factor_c.T, factor_c, precision=precise, preferred_element_type=jnp.float32)
        contracted = jnp.einsum('ijk,kr->ijr', intensities, factor_c, precision=precise)
        drive_a = jnp.einsum('ijr,jr->ir', contracted, factor_b, precision=precise)
        drive_b = jnp.einsum('ijr,ir->jr', contracted, factor_a, precision=precise)
        khatri_rao = (factor_a[:, None, :] * factor_b[None, :, :]).reshape(SAMPLES * SCANS, RANK)
        drive_c = lax.dot_general(unfolded, khatri_rao, (((0,), (0,)), ((), ())), precision=precise, preferred_element_type=jnp.float32)
        hessian_a = gram_b * gram_c
        hessian_b = gram_a * gram_c
        hessian_c = gram_a * gram_b
        new_a = factor_a - (jnp.dot(factor_a, hessian_a, precision=precise, preferred_element_type=jnp.float32) - drive_a) / frobenius(hessian_a)
        new_b = factor_b - (jnp.dot(factor_b, hessian_b, precision=precise, preferred_element_type=jnp.float32) - drive_b) / frobenius(hessian_b)
        new_c = factor_c - (jnp.dot(factor_c, hessian_c, precision=precise, preferred_element_type=jnp.float32) - drive_c) / frobenius(hessian_c)
        factor_a, factor_b, factor_c = (new_a, new_b, new_c)
    return (factor_a, factor_b, factor_c)
```

```python
import functools

import jax
import jax.numpy as jnp
from jax import lax
from jax.experimental import pallas as pl
from jax.experimental.pallas import tpu as pltpu
from jax.sharding import PartitionSpec as P

STEPS = 2
UNIT = 256
PAIR = 2 * UNIT
FIRST = (1, 3, 4)
LAST = (4, 2, 1, 1)
F32 = jnp.float32
BF16 = jnp.bfloat16
VMEM_LIMIT = 36 << 20
NOWHERE = pl.BlockSpec(memory_space=pl.ANY)
HELD = pl.BlockSpec(memory_space=pltpu.VMEM)


def split(value):
    high = value.astype(BF16)
    return high, (value - high.astype(F32)).astype(BF16)


def plain(a, b):
    return jnp.dot(a, b, preferred_element_type=F32)


def dot(a, b):
    a_high, a_low = split(a)
    b_high, b_low = split(b)
    return plain(a_high, b_high) + (plain(a_high, b_low) + plain(a_low, b_high))


def gram(factor):
    return dot(factor.T, factor)


def inverse_norm(matrix):
    return 1.0 / jnp.sqrt(jnp.sum(matrix * matrix, keepdims=True) + 1e-12)


def in_vmem(value):
    return pltpu.with_memory_space_constraint(value, pltpu.VMEM)


def params():
    return pltpu.CompilerParams(vmem_limit_bytes=VMEM_LIMIT)


def shaped(*dims):
    return jax.ShapeDtypeStruct(dims, F32)


def whole(shape):
    return pl.BlockSpec(shape, lambda *_: (0,) * len(shape))


def rows_block(rows, rank, start=0):
    return pl.BlockSpec((rows, rank), lambda j, *_: (start + j, 0))


def call(kernel, name, grid, in_specs, out_specs, out_shape, scratch=(), aliases=None):
    return pl.pallas_call(
        kernel,
        grid_spec=pltpu.PrefetchScalarGridSpec(
            num_scalar_prefetch=1,
            grid=grid,
            in_specs=in_specs,
            out_specs=out_specs,
            scratch_shapes=scratch,
        ),
        out_shape=out_shape,
        input_output_aliases=aliases or {},
        cost_estimate=pl.CostEstimate(flops=0, bytes_accessed=0, transcendentals=0),
        compiler_params=params(),
        name=name,
    )


def fill_khatri_rao(krt_ref, a, b):
    rank = a.shape[1]
    product = (a[:, None, :] * b[None, :, :]).reshape(-1, rank).T
    krt_ref[:rank], krt_ref[rank:] = split(product)


def mass_part(krt_ref, x_high, x_low):
    rank = krt_ref.shape[0] // 2
    both = plain(krt_ref[...], x_high)
    return (both[:rank] + (both[rank:] + plain(krt_ref[:rank], x_low))).T


def store_sides(core, out, theirs_ref, mine_ref):
    at_zero = core == 0
    theirs_ref[...] = jnp.where(at_zero, out[UNIT:], out[:UNIT])
    mine_ref[...] = jnp.where(at_zero, out[:UNIT], out[UNIT:])


def contract(x_high, x_low, c):
    rank = c.shape[1]
    c_high, c_low = split(c)
    both = plain(x_high, jnp.concatenate([c_high, c_low], 1))
    return both[:, :rank] + (both[:, rank:] + plain(x_low, c_high))


def store_drives(out_ref, total, a, b):
    rows = a.shape[0]
    folded = total.reshape(rows, b.shape[0], a.shape[1])
    out_ref[:rows] = jnp.sum(folded * b[None], 1)
    out_ref[rows : rows + b.shape[0]] = jnp.sum(folded * a[:, None, :], 0)


def sides(core, mine, theirs):
    at_zero = core == 0
    return jnp.concatenate([jnp.where(at_zero, mine, theirs), jnp.where(at_zero, theirs, mine)], 0)


def add_half_gram(out_ref, core, factor):
    half = factor.shape[1] // 2
    out_ref[-half:] += dot(jnp.where(core == 0, factor[:, :half], factor[:, half:]).T, factor)


def load_kernel(core_ref, a_ref, b_ref, x_ref, c_ref, high_ref, low_ref, krt_ref, out_ref, total_ref):
    step = pl.program_id(0)

    @pl.when(step == 0)
    def _():
        total_ref[...] = jnp.zeros_like(total_ref)
        out_ref[...] = jnp.zeros_like(out_ref)
        fill_khatri_rao(krt_ref, a_ref[...], b_ref[...])

    x_high, x_low = split(x_ref[...])
    high_ref[step] = x_high
    low_ref[step] = x_low
    c = c_ref[...]
    total_ref[...] += contract(x_high, x_low, c)
    add_half_gram(out_ref, core_ref[0], c)

    @pl.when(step == pl.num_programs(0) - 1)
    def _():
        store_drives(out_ref, total_ref[...], a_ref[...], b_ref[...])


def load(core, a, b, x, c):
    rows, bins = x.shape
    rank = c.shape[1]
    units = bins // PAIR
    out = shaped(a.shape[0] + b.shape[0] + rank // 2, rank)
    part = pltpu.VMEM((units, rows, PAIR), BF16)
    return call(
        load_kernel,
        "load",
        (units,),
        [
            whole(a.shape),
            whole(b.shape),
            pl.BlockSpec((rows, PAIR), lambda j, core_ref: (0, j)),
            rows_block(PAIR, rank),
        ],
        [HELD, HELD, HELD, whole(out.shape)],
        (part, part, pltpu.VMEM((2 * rank, rows), BF16), out),
        [pltpu.VMEM((rows, rank), F32)],
    )(core, a, b, pltpu.with_memory_space_constraint(x, pltpu.HBM), c)


def mass_kernel(start, core_ref, krt_ref, high_ref, low_ref, *refs):
    theirs_ref, mine_ref = refs[-2:]
    unit = start + pl.program_id(0)
    out = mass_part(krt_ref, high_ref[unit], low_ref[unit])
    store_sides(core_ref[0], out, theirs_ref, mine_ref)


def mass_products(core, krt, parts, after, start, units):
    rank = krt.shape[0] // 2
    out = shaped(units * UNIT, rank)
    side = rows_block(UNIT, rank)
    return call(
        functools.partial(mass_kernel, start),
        "mass_products",
        (units,),
        [HELD, HELD, HELD] + [NOWHERE] * len(after),
        [side, side],
        (out, out),
    )(core, in_vmem(krt), in_vmem(parts[0]), in_vmem(parts[1]), *after)


def drive_kernel(start, started, last, core_ref, a_ref, b_ref, hessian_ref, high_ref, low_ref, c_ref, mine_ref, theirs_ref, held_ref, gram_ref, *refs):
    new_ref, out_ref, out_gram_ref, total_ref = refs
    step = pl.program_id(0)
    core = core_ref[0]

    @pl.when(step == 0)
    def _():
        total_ref[...] = held_ref[...] if started else jnp.zeros_like(total_ref)
        out_gram_ref[...] = gram_ref[...] if started else jnp.zeros_like(out_gram_ref)

    new = mass_new(hessian_ref, c_ref[...], sides(core, mine_ref[...], theirs_ref[...]))
    new_ref[...] = new
    unit = start + step
    total_ref[...] += contract(high_ref[unit], low_ref[unit], new)
    add_half_gram(out_gram_ref, core, new)

    @pl.when(step == pl.num_programs(0) - 1)
    def _():
        if last:
            store_drives(out_ref, total_ref[...], a_ref[...], b_ref[...])
        else:
            out_ref[...] = total_ref[...]


def drive_products(core, a, b, hessian, parts, c, mine, theirs, held, start, last):
    rank = a.shape[1]
    rows = a.shape[0] * b.shape[0]
    units = mine.shape[0] // UNIT
    side = rows_block(UNIT, rank)
    half = shaped(rank // 2, rank)
    out = shaped(a.shape[0] + b.shape[0], rank) if last else shaped(rows, rank)
    started = held is not None
    new = shaped(units * PAIR, rank)
    total, gram_held = held if started else (mine, mine)
    return call(
        functools.partial(drive_kernel, start, started, last),
        "drive_products",
        (units,),
        [
            whole(a.shape),
            whole(b.shape),
            whole(hessian.shape),
            HELD,
            HELD,
            rows_block(PAIR, rank, start),
            side,
            side,
            whole((rows, rank)) if started else NOWHERE,
            whole(half.shape) if started else NOWHERE,
        ],
        [rows_block(PAIR, rank), whole(out.shape), whole(half.shape)],
        (new, out, half),
        [pltpu.VMEM((rows, rank), F32)],
    )(core, a, b, hessian, in_vmem(parts[0]), in_vmem(parts[1]), c, mine, theirs, total, gram_held)


def mass_new(hessian_ref, c, total):
    rank = c.shape[1]
    return c - dot(c, hessian_ref[:rank]) + total * hessian_ref[rank:, :1][:1]


def last_kernel(core_ref, hessian_ref, c_ref, mine_ref, theirs_ref, held_ref, out_ref):
    total = sides(core_ref[0], mine_ref[...], theirs_ref[...])
    out_ref[...] = mass_new(hessian_ref, c_ref[...], total)


def last_step(core, hessian, c, c_start, mine, theirs, held, start, bins):
    rank = c.shape[1]
    side = rows_block(UNIT, rank)
    first = held is None
    return call(
        last_kernel,
        "last_step",
        (mine.shape[0] // UNIT,),
        [whole(hessian.shape), rows_block(PAIR, rank, c_start), side, side, NOWHERE],
        rows_block(PAIR, rank, start),
        shaped(bins, rank),
        (),
        {} if first else {5: 0},
    )(core, hessian, c, mine, theirs, mine if first else held)


def sample_gram_kernel(core_ref, a_ref, far_ref, out_ref):
    out_ref[...] = gram(a_ref[...]) + gram(far_ref[...])


def sample_gram(core, a, far):
    rank = a.shape[1]
    return call(
        sample_gram_kernel,
        "sample_gram",
        (1,),
        [whole(a.shape), whole(a.shape)],
        whole((rank, rank)),
        shaped(rank, rank),
    )(core, a, far)


def hessian_kernel(core_ref, gram_ref, other_ref, b_ref, out_ref):
    rank = gram_ref.shape[0]
    hessian = (gram_ref[...] + other_ref[...]) * gram(b_ref[...])
    scale = inverse_norm(hessian)
    out_ref[:rank] = hessian * scale
    out_ref[rank:] = jnp.broadcast_to(scale, (8, rank))


def mass_hessian(core, gram_a, gram_a_other, b):
    rank = b.shape[1]
    square = whole((rank, rank))
    return call(
        hessian_kernel,
        "mass_hessian",
        (1,),
        [square, square, whole(b.shape)],
        whole((rank + 8, rank)),
        shaped(rank + 8, rank),
    )(core, gram_a, gram_a_other, b)


def small_step_kernel(
    core_ref,
    a_ref,
    b_ref,
    gram_a_ref,
    gram_a_other_ref,
    gram_c_ref,
    gram_c_other_ref,
    drive_ref,
    drive_far_ref,
    drive_b_ref,
    drive_b_far_ref,
    after_ref,
    new_a_ref,
    new_b_ref,
    *refs,
):
    a, b = a_ref[...], b_ref[...]
    rows = a.shape[0]
    scans = b.shape[0]
    gram_a = gram_a_ref[...] + gram_a_other_ref[...]
    gram_c = sides(core_ref[0], gram_c_ref[scans:], gram_c_other_ref[scans:])
    hessian_a = gram(b) * gram_c
    hessian_b = gram_a * gram_c
    drive_a = drive_ref[:rows] + drive_far_ref[:rows]
    drive_b = drive_b_ref[...] + drive_b_far_ref[...]
    new_a = a - (dot(a, hessian_a) - drive_a) * inverse_norm(hessian_a)
    new_b = b - (dot(b, hessian_b) - drive_b) * inverse_norm(hessian_b)
    new_a_ref[...] = new_a
    new_b_ref[...] = new_b
    if refs:
        fill_khatri_rao(refs[0], new_a, new_b)


def small_step(core, a, b, args, after, last):
    outs = [shaped(*a.shape), shaped(*b.shape)]
    specs = [whole(a.shape), whole(b.shape)]
    if not last:
        outs.append(pltpu.VMEM((2 * a.shape[1], a.shape[0] * b.shape[0]), BF16))
        specs.append(HELD)
    return call(
        small_step_kernel,
        "small_step",
        (1,),
        [whole(v.shape) for v in (a, b, *args)] + [NOWHERE],
        specs,
        outs,
    )(core, a, b, *args, after)


def swap(value, axis, size, distance):
    return lax.ppermute(value, axis, [(i, i ^ distance) for i in range(size)])


def local(mz, intensities, sample_start, scan_start, mass_start):
    a, b, c = sample_start, scan_start, mass_start
    bins, rank = c.shape
    rows, scans = a.shape[0], b.shape[0]
    x = intensities.reshape(-1, bins)
    core = (lax.axis_index("grp") % 2).reshape(1).astype(jnp.int32)

    def over_core(value):
        return swap(value, "grp", 4, 1)

    def over_x(value):
        return swap(value, "grp", 4, 2)

    def sum_mz(value):
        distance = 1
        while True:
            far = swap(value, "mz", mz, distance)
            distance *= 2
            if distance >= mz:
                return value, far
            value = value + far

    def close_drives(packed):
        packed, far = sum_mz(packed)
        tail = packed[rows:] + far[rows:]
        other = over_core(tail)
        drive_b = tail[:scans] + other[:scans]
        return tail, other, packed, far, drive_b, over_x(drive_b)

    high, low, krt, packed = load(core, a, b, x, c)
    parts = high, low
    sums = []
    after = (packed,)
    start = 0
    for number, units in enumerate(FIRST):
        theirs, mine = mass_products(core, krt, parts, after, start, units)
        after = (mine,)
        total = mine + over_core(theirs)
        if number == 0:
            total = jnp.concatenate([total, a], 0)
        far = over_x(total)
        if number == 0:
            gram_a = sample_gram(core, a, far[units * UNIT :])
            gram_a = gram_a, over_core(gram_a)
        sums.append((start, total[: units * UNIT] + far[: units * UNIT]))
        start += units
    small = close_drives(packed)
    hessian = mass_hessian(core, *gram_a, b)
    held = None
    firsts = []
    for start, total in sums[:-1]:
        new, *held = drive_products(
            core, a, b, hessian, parts, c, total, over_core(total), held, start, False
        )
        firsts.append((start, new))
    a, b, krt = small_step(core, a, b, (*gram_a, *small), held[0], False)

    lasts = []
    after = ()
    first = 0
    for number, units in enumerate(LAST):
        theirs, mine = mass_products(core, krt, parts, after, first, units)
        after = (mine,)
        total = mine + over_core(theirs)
        if number == 0:
            total = jnp.concatenate([total, a], 0)
        far = over_x(total)
        if number == 0:
            gram_a = sample_gram(core, a, far[units * UNIT :])
            gram_a = gram_a, over_core(gram_a)
        lasts.append((first, units, total[: units * UNIT] + far[: units * UNIT]))
        first += units
    start, total = sums[-1]
    new, *packed = drive_products(
        core, a, b, hessian, parts, c, total, over_core(total), held, start, True
    )
    firsts.append((start, new))
    small = close_drives(jnp.concatenate(packed, 0))
    hessian = mass_hessian(core, *gram_a, b)
    out = None
    for start, units, total in lasts:
        other = over_core(total)
        done = 0
        while done < units:
            begin, new = [v for v in firsts if v[0] <= start + done][-1]
            here = min(units - done, begin + new.shape[0] // PAIR - start - done)
            part = slice(done * UNIT, (done + here) * UNIT)
            whole_chunk = here == units
            out = last_step(
                core,
                hessian,
                new,
                start + done - begin,
                total if whole_chunk else total[part],
                other if whole_chunk else other[part],
                out,
                start + done,
                bins,
            )
            done += here
    new_a, new_b = small_step(core, a, b, (*gram_a, *small), a, True)
    return new_a, new_b, out


def solution(mesh):
    placed = (P("grp", None, "mz"), P("grp", None), P(), P("mz", None))
    return jax.shard_map(
        functools.partial(local, mesh.shape["mz"]),
        mesh=mesh,
        in_specs=placed,
        out_specs=(P("grp", None), P(), P("mz", None)),
        check_vma=False,
    )
```

```python
import functools

import jax
import jax.numpy as jnp
from jax import lax
from jax.experimental import pallas as pl
from jax.experimental.pallas import tpu as pltpu
from jax.sharding import PartitionSpec as P

STEPS = 2
UNIT = 256
PAIR = 2 * UNIT
FIRST = (False, True, True, False)
LAST = ((0, 0, 2), (1, 0, 2), (2, 0, 2), (3, 0, 2))
F32 = jnp.float32
BF16 = jnp.bfloat16
VMEM_LIMIT = 6 << 20
LOAD_VMEM_LIMIT = 20 << 20
NOWHERE = pl.BlockSpec(memory_space=pl.ANY)
HELD = pl.BlockSpec(memory_space=pltpu.VMEM)


def split(value):
    high = value.astype(BF16)
    return high, (value - high.astype(F32)).astype(BF16)


def plain(a, b):
    return jnp.dot(a, b, preferred_element_type=F32)


def dot(a, b):
    a_high, a_low = split(a)
    b_high, b_low = split(b)
    return plain(a_high, b_high) + (plain(a_high, b_low) + plain(a_low, b_high))


def gram(factor):
    return dot(factor.T, factor)


def inverse_norm(matrix):
    return 1.0 / jnp.sqrt(jnp.sum(matrix * matrix, keepdims=True) + 1e-12)


def in_vmem(value):
    return pltpu.with_memory_space_constraint(value, pltpu.VMEM)


def shaped(*dims):
    return jax.ShapeDtypeStruct(dims, F32)


def whole(shape):
    return pl.BlockSpec(shape, lambda *_: (0,) * len(shape))


def in_hbm(value):
    return pltpu.with_memory_space_constraint(value, pltpu.HBM)


def rows_block(rows, rank, start=0):
    return pl.BlockSpec((rows, rank), lambda j, *_: (start + j, 0))


def call(kernel, name, grid, in_specs, out_specs, out_shape, scratch=(), aliases=None, kept=()):
    inputs = len(in_specs)

    def without_kept(core_ref, *refs):
        kernel(core_ref, *refs[:inputs], *refs[inputs + len(kept) :])

    run = pl.pallas_call(
        without_kept if kept else kernel,
        grid_spec=pltpu.PrefetchScalarGridSpec(
            num_scalar_prefetch=1,
            grid=grid,
            in_specs=list(in_specs) + [HELD for _ in kept],
            out_specs=out_specs,
            scratch_shapes=scratch,
        ),
        out_shape=out_shape,
        input_output_aliases=aliases or {},
        cost_estimate=pl.CostEstimate(flops=0, bytes_accessed=0, transcendentals=0),
        compiler_params=pltpu.CompilerParams(
            vmem_limit_bytes=LOAD_VMEM_LIMIT if name in ("load", "first_products") else VMEM_LIMIT
        ),
        name=name,
    )
    return lambda *args: run(*args, *(in_vmem(value) for value in kept))


def give_kernel(start, core_ref, x_ref, after_ref, out_ref, sem):
    bins = x_ref.shape[1]
    column = (1 - core_ref[0]) * (bins // 2) + start * PAIR
    copy = pltpu.make_async_copy(
        x_ref.at[:, pl.ds(pl.multiple_of(column, PAIR), PAIR)], out_ref, sem
    )
    copy.start()
    copy.wait()


def give(core, x, after, start):
    return call(
        functools.partial(give_kernel, start),
        "give",
        (1,),
        [NOWHERE, NOWHERE],
        HELD,
        pltpu.VMEM((x.shape[0], PAIR), F32),
        [pltpu.SemaphoreType.DMA],
    )(core, in_hbm(x), after)


def add_kernel(core_ref, near_ref, far_ref, *refs):
    refs[-1][...] = near_ref[...] + far_ref[...]


def add(core, near, far, after, kept):
    block = whole(near.shape)
    return call(
        add_kernel,
        "add",
        (1,),
        [block, block] + [NOWHERE for _ in after],
        block,
        shaped(*near.shape),
        kept=kept,
    )(core, near, far, *after)


def fill_khatri_rao(krt_ref, a, b):
    rank = a.shape[1]
    product = (a[:, None, :] * b[None, :, :]).reshape(-1, rank).T
    krt_ref[:rank], krt_ref[rank:] = split(product)


def mass_part(krt_ref, x_high, x_low):
    rank = krt_ref.shape[0] // 2
    both = plain(krt_ref[...], x_high)
    return (both[:rank] + (both[rank:] + plain(krt_ref[:rank], x_low))).T


def contract(x_high, x_low, c):
    rank = c.shape[1]
    c_high, c_low = split(c)
    both = plain(x_high, jnp.concatenate([c_high, c_low], 1))
    return both[:, :rank] + (both[:, rank:] + plain(x_low, c_high))


def store_sums(core, keep_ref, send_ref, total, squares, a, b):
    both = a.shape[0]
    rows, scans, half = both // 2, b.shape[0], squares.shape[0] // 2
    folded = total.reshape(both, scans, a.shape[1])
    drive = jnp.sum(folded * b[None], 1)
    drive_b = jnp.sum(folded * a[:, None, :], 0)
    keep_ref[:rows], send_ref[:rows] = drive[:rows], drive[rows:]
    keep_ref[rows : rows + scans] = drive_b
    send_ref[rows : rows + scans] = drive_b
    at_zero = core == 0
    keep_ref[rows + scans :] = jnp.where(at_zero, squares[:half], squares[half:])
    send_ref[rows + scans :] = jnp.where(at_zero, squares[half:], squares[:half])


def load_kernel(started, last, with_mass, core_ref, a_ref, b_ref, x_ref, other_ref, c_ref, krt_in_ref, total_in_ref, gram_in_ref, after_ref, *refs):
    high_ref, low_ref, *refs = refs
    if with_mass:
        mass_ref, *refs = refs
    if last:
        keep_ref, send_ref, *refs = refs
    total_ref, gram_ref, *refs = refs
    krt_ref = krt_in_ref if started else refs[0]
    step = pl.program_id(0)
    rows = x_ref.shape[0]

    @pl.when(step == 0)
    def _():
        total_ref[...] = total_in_ref[...] if started else jnp.zeros_like(total_ref)
        gram_ref[...] = gram_in_ref[...] if started else jnp.zeros_like(gram_ref)
        if not started:
            fill_khatri_rao(krt_ref, a_ref[...], b_ref[...])

    high_ref[step, :rows], low_ref[step, :rows] = split(x_ref[...])
    high_ref[step, rows:], low_ref[step, rows:] = split(other_ref[...])
    x_high, x_low = high_ref[step], low_ref[step]
    if with_mass:
        mass_ref[...] = mass_part(krt_ref, x_high, x_low)
    c = c_ref[...]
    total_ref[...] += contract(x_high, x_low, c)
    gram_ref[...] += gram(c)

    if last:

        @pl.when(step == pl.num_programs(0) - 1)
        def _():
            store_sums(
                core_ref[0], keep_ref, send_ref, total_ref[...], gram_ref[...], a_ref[...], b_ref[...]
            )


def load(core, a, b, x, other, c, krt, held, after, kept, start, last, with_mass):
    rows, bins = x.shape
    rank = c.shape[1]
    blocks = bins // (2 * PAIR)
    started = held is not None
    units = other.shape[1] // PAIR
    part = pltpu.VMEM((units, 2 * rows, PAIR), BF16)
    mass = [shaped(units * PAIR, rank)] if with_mass else []
    total, squares = shaped(2 * rows, rank), shaped(rank, rank)
    sums = shaped(a.shape[0] // 2 + b.shape[0] + rank // 2, rank)
    tail = [sums, sums] if last else [pltpu.VMEM(total.shape, F32), squares]
    tail_specs = [whole(sums.shape)] * 2 if last else [HELD, whole(squares.shape)]
    if not started:
        tail.append(pltpu.VMEM((2 * rank, 2 * rows), BF16))
        tail_specs.append(HELD)
    return call(
        functools.partial(load_kernel, started, last, with_mass),
        "load",
        (units,),
        [
            whole(a.shape),
            whole(b.shape),
            pl.BlockSpec((rows, PAIR), lambda j, core_ref: (0, core_ref[0] * blocks + start + j)),
            pl.BlockSpec((rows, PAIR), lambda j, core_ref: (0, j)),
            pl.BlockSpec((PAIR, rank), lambda j, core_ref: (core_ref[0] * blocks + start + j, 0)),
            HELD if started else NOWHERE,
            HELD if started else NOWHERE,
            whole(squares.shape) if started else NOWHERE,
            NOWHERE,
        ],
        [HELD, HELD] + [rows_block(PAIR, rank) for _ in mass] + tail_specs,
        [part, part] + mass + tail,
        [pltpu.VMEM(total.shape, F32), pltpu.VMEM(squares.shape, F32)] if last else [],
        kept=kept,
    )(
        core,
        a,
        b,
        in_hbm(x),
        in_hbm(other) if not started else other,
        in_hbm(c),
        in_vmem(krt) if started else after,
        in_vmem(held[0]) if started else after,
        held[1] if started else after,
        after,
    )


def first_kernel(core_ref, a_ref, b_ref, x_ref, other_ref, after_ref, out_ref, krt_ref):
    fill_khatri_rao(krt_ref, a_ref[...], b_ref[...])
    x_high, x_low = split(jnp.concatenate([x_ref[...], other_ref[...]], 0))
    out_ref[...] = mass_part(krt_ref, x_high, x_low)


def first_products(core, a, b, x, other, after):
    rows, bins = x.shape
    rank = a.shape[1]
    blocks = bins // (2 * PAIR)
    return call(
        first_kernel,
        "first_products",
        (1,),
        [
            whole(a.shape),
            whole(b.shape),
            pl.BlockSpec((rows, PAIR), lambda j, core_ref: (0, core_ref[0] * blocks)),
            whole(other.shape),
            NOWHERE,
        ],
        whole((PAIR, rank)),
        shaped(PAIR, rank),
        [pltpu.VMEM((2 * rank, 2 * rows), BF16)],
    )(core, a, b, in_hbm(x), other, after)


def mass_kernel(start, core_ref, krt_ref, high_ref, low_ref, after_ref, out_ref):
    unit = start + pl.program_id(0)
    columns = pl.ds(pl.multiple_of(unit % 2 * UNIT, UNIT), UNIT)
    out_ref[...] = mass_part(krt_ref, high_ref[unit // 2, :, columns], low_ref[unit // 2, :, columns])


def mass_products(core, krt, parts, after, kept, start, units):
    rank = krt.shape[0] // 2
    return call(
        functools.partial(mass_kernel, start),
        "mass_products",
        (units,),
        [HELD, HELD, HELD, NOWHERE],
        rows_block(UNIT, rank),
        shaped(units * UNIT, rank),
        kept=kept,
    )(core, in_vmem(krt), in_vmem(parts[0]), in_vmem(parts[1]), after)


def drive_kernel(start, started, last, core_ref, a_ref, b_ref, scale_ref, high_ref, low_ref, base_ref, near_ref, far_ref, total_in_ref, gram_in_ref, after_ref, *refs):
    if last:
        new_ref, keep_ref, send_ref, total_ref, gram_ref = refs
    else:
        new_ref, total_ref, gram_ref = refs
    step = pl.program_id(0)

    @pl.when(step == 0)
    def _():
        total_ref[...] = total_in_ref[...] if started else jnp.zeros_like(total_ref)
        gram_ref[...] = gram_in_ref[...] if started else jnp.zeros_like(gram_ref)

    place = pl.ds(pl.multiple_of((start + step) * PAIR, PAIR), PAIR)
    new = base_ref[place] + (near_ref[...] + far_ref[...]) * scale_ref[:1, :1]
    new_ref[pl.ds(pl.multiple_of(step * PAIR, PAIR), PAIR)] = new
    total_ref[...] += contract(high_ref[step], low_ref[step], new)
    gram_ref[...] += gram(new)

    if last:

        @pl.when(step == pl.num_programs(0) - 1)
        def _():
            store_sums(
                core_ref[0], keep_ref, send_ref, total_ref[...], gram_ref[...], a_ref[...], b_ref[...]
            )


def drive_products(core, a, b, scale, parts, base, near, far, held, after, kept, start, last):
    rank = a.shape[1]
    units, rows = parts[0].shape[:2]
    started = held is not None
    total, squares = shaped(rows, rank), shaped(rank, rank)
    sums = shaped(a.shape[0] // 2 + b.shape[0] + rank // 2, rank)
    tail = [sums, sums] if last else [pltpu.VMEM(total.shape, F32), squares]
    tail_specs = [whole(sums.shape)] * 2 if last else [HELD, whole(squares.shape)]
    return call(
        functools.partial(drive_kernel, start, started, last),
        "drive_products",
        (units,),
        [
            whole(a.shape),
            whole(b.shape),
            whole(scale.shape),
            HELD,
            HELD,
            HELD,
            rows_block(PAIR, rank),
            rows_block(PAIR, rank),
            HELD if started else NOWHERE,
            whole(squares.shape) if started else NOWHERE,
            NOWHERE,
        ],
        [HELD] + tail_specs,
        [pltpu.VMEM((units * PAIR, rank), F32)] + tail,
        [pltpu.VMEM(total.shape, F32), pltpu.VMEM(squares.shape, F32)] if last else [],
        kept=kept,
    )(
        core,
        a,
        b,
        scale,
        in_vmem(parts[0]),
        in_vmem(parts[1]),
        in_vmem(base),
        near,
        far,
        in_vmem(held[0]) if started else after,
        held[1] if started else after,
        after,
    )


def base_kernel(core_ref, gram_ref, other_ref, b_ref, after_ref, *refs):
    out_ref, scale_ref = refs[-2:]
    hessian = (gram_ref[...] + other_ref[...]) * gram(b_ref[...])
    scale = inverse_norm(hessian)
    hessian = hessian * scale
    scale_ref[...] = jnp.broadcast_to(scale, scale_ref.shape)
    done = 0
    for c_ref in refs[:-2]:
        for start in range(0, c_ref.shape[0], PAIR):
            c = c_ref[start : start + PAIR]
            out_ref[done : done + PAIR] = c - dot(c, hessian)
            done += PAIR


def mass_base(core, gram_a, gram_a_other, b, pieces, after, kept):
    rank = b.shape[1]
    square = whole((rank, rank))
    scale = shaped(8, rank)
    bins = sum(piece.shape[0] for piece in pieces)
    return call(
        base_kernel,
        "mass_base",
        (1,),
        [square, square, whole(b.shape), NOWHERE] + [HELD for _ in pieces],
        [HELD, whole(scale.shape)],
        (pltpu.VMEM((bins, rank), F32), scale),
        kept=kept,
    )(core, gram_a, gram_a_other, b, after, *(in_vmem(piece) for piece in pieces))


def last_kernel(start, core_ref, scale_ref, base_ref, near_ref, far_ref, *refs):
    place = pl.ds(pl.multiple_of((start + pl.program_id(0)) * UNIT, UNIT), UNIT)
    refs[-1][...] = base_ref[place] + (near_ref[...] + far_ref[...]) * scale_ref[:1, :1]


def last_step(core, scale, base, near, far, after, start):
    rank = base.shape[1]
    side = rows_block(UNIT, rank)
    return call(
        functools.partial(last_kernel, start),
        "last_step",
        (near.shape[0] // UNIT,),
        [whole(scale.shape), HELD, side, side] + [NOWHERE for _ in after],
        side,
        shaped(*near.shape),
    )(core, scale, in_vmem(base), near, far, *after)


def join_kernel(core_ref, mine_ref, theirs_ref, held_ref, after_ref, out_ref, done_ref):
    done_ref[...] = jnp.zeros_like(done_ref)

    @pl.when(pl.program_id(0) == 0)
    def _():
        out_ref[...] = mine_ref[...]

    @pl.when(pl.program_id(0) == 1)
    def _():
        out_ref[...] = theirs_ref[...]


def join(core, mine, theirs, held, after, chunk, bins):
    rows, rank = mine.shape
    chunks = bins // (2 * rows)
    first = held is None

    def place(side, core_ref):
        return jnp.where(side == 0, core_ref[0], 1 - core_ref[0]) * chunks + chunk, 0

    return call(
        join_kernel,
        "join",
        (2,),
        [whole(mine.shape), whole(mine.shape), NOWHERE, NOWHERE],
        [pl.BlockSpec((rows, rank), place), whole((8, 128))],
        (shaped(bins, rank), shaped(8, 128)),
        (),
        {} if first else {3: 0},
    )(core, mine, theirs, mine if first else held, after)


def sample_gram_kernel(core_ref, a_ref, far_ref, after_ref, out_ref):
    out_ref[...] = gram(a_ref[...]) + gram(far_ref[...])


def sample_gram(core, a, far, after, kept):
    rank = a.shape[1]
    return call(
        sample_gram_kernel,
        "sample_gram",
        (1,),
        [whole(a.shape), whole(a.shape), NOWHERE],
        whole((rank, rank)),
        shaped(rank, rank),
        kept=kept,
    )(core, a, far, after)


def small_step_kernel(
    core_ref,
    a_ref,
    b_ref,
    gram_a_ref,
    gram_a_other_ref,
    gram_c_ref,
    gram_c_other_ref,
    drive_ref,
    drive_other_ref,
    drive_b_ref,
    drive_b_far_ref,
    after_ref,
    new_a_ref,
    new_b_ref,
    *refs,
):
    a, b = a_ref[...], b_ref[...]
    gram_a = gram_a_ref[...] + gram_a_other_ref[...]
    at_zero = core_ref[0] == 0
    mine, other = gram_c_ref[...], gram_c_other_ref[...]
    gram_c = jnp.concatenate([jnp.where(at_zero, mine, other), jnp.where(at_zero, other, mine)], 0)
    hessian_a = gram(b) * gram_c
    hessian_b = gram_a * gram_c
    drive_a = jnp.concatenate([drive_ref[...], drive_other_ref[...]], 0)
    drive_b = drive_b_ref[...] + drive_b_far_ref[...]
    new_a = a - (dot(a, hessian_a) - drive_a) * inverse_norm(hessian_a)
    new_b = b - (dot(b, hessian_b) - drive_b) * inverse_norm(hessian_b)
    new_a_ref[...] = new_a[: new_a_ref.shape[0]]
    new_b_ref[...] = new_b
    if refs:
        fill_khatri_rao(refs[0], new_a, new_b)


def small_step(core, a, b, args, after, kept, last):
    rows = a.shape[0] // 2 if last else a.shape[0]
    outs = [shaped(rows, a.shape[1]), shaped(*b.shape)]
    specs = [whole(outs[0].shape), whole(b.shape)]
    if not last:
        outs.append(pltpu.VMEM((2 * a.shape[1], a.shape[0] * b.shape[0]), BF16))
        specs.append(HELD)
    return call(
        small_step_kernel,
        "small_step",
        (1,),
        [whole(v.shape) for v in (a, b, *args)] + [NOWHERE],
        specs,
        outs,
        kept=kept,
    )(core, a, b, *args, after)


def swap(value, axis, size, distance):
    return lax.ppermute(value, axis, [(i, i ^ distance) for i in range(size)])


def local(mz, intensities, sample_start, scan_start, mass_start):
    b, c = scan_start, mass_start
    bins, rank = c.shape
    rows, scans = sample_start.shape[0], b.shape[0]
    x = intensities.reshape(-1, bins)
    number = lax.axis_index("grp") % 2
    core = number.reshape(1).astype(jnp.int32)

    def over_core(value):
        return swap(value, "grp", 4, 1)

    def over_x(value):
        return swap(value, "grp", 4, 2)

    def sum_mz(value, first, befores, kept, done=0):
        values = []
        distances = [1 << i for i in range(mz.bit_length() - 1)]
        place = distances.index(first)
        for distance in (distances[place:] + distances[:place])[: len(distances) - done]:
            far = swap(value, "mz", mz, distance)
            after, *befores = befores or [None]
            value = value + far if after is None else add(core, value, far, (after,), kept)
            values.append(value)
        return value, values[0]

    def close(keep, send, before, befores, kept):
        total = add(core, keep, over_core(send), before, kept)
        gram_c, _ = sum_mz(total[rows + scans :], mz // 2, [], kept)
        drive, early = sum_mz(total[: rows + scans], 1, befores, kept)
        drive, drive_b = drive[:rows], drive[rows:]
        return (gram_c, over_core(gram_c), drive, over_core(drive), drive_b, over_x(drive_b)), early

    def grams(a, far, after, kept):
        part = sample_gram(core, a[:rows], far, after, kept)
        return part, over_core(part)

    places = range(len(FIRST))
    others, after = [], x
    for place in places[:2]:
        after = give(core, x, after, place)
        others.append(over_core(after))
    a = jnp.concatenate([sample_start, over_core(sample_start)], 0)
    far_a = over_x(sample_start)

    parts, nears = [], [first_products(core, a, b, x, others[0], after)]
    kept = ()
    after = nears[0]
    for place in places[2:]:
        after = give(core, x, after, place)
        others.append(over_core(after))
    krt, held = None, None
    for place in places:
        high, low, *rest = load(
            core, a, b, x, others[place], c, krt, held, after, kept, place, place == places[-1], FIRST[place]
        )
        if FIRST[place]:
            after, *rest = rest
            nears.append(after)
        if krt is None:
            krt = rest.pop()
        held = rest
        parts.append((high, low))
        kept += (high, low)
        if place == places[-1]:
            gram_a = grams(a, far_a, held[0], kept)
            c_mine = lax.dynamic_slice_in_dim(c, number * (bins // 2), bins // 2, 0)
            base, scale = mass_base(core, *gram_a, b, [c_mine], after, kept)

    fars = [over_x(near) for near in nears]
    news, sums = [], None
    kept_base = kept + (base,)

    def drives(place, after):
        nonlocal sums
        new, *sums = drive_products(
            core,
            a,
            b,
            scale,
            parts[place],
            base,
            nears[place],
            fars[place],
            sums,
            after,
            kept,
            place,
            place == places[-1],
        )
        news.append(new)
        return new

    old_a = a
    after = held[0]
    for place in places[len(nears) :]:
        after = mass_products(core, krt, parts[place], after, kept_base, 0, 2)
        nears.append(after)
        fars.append(over_x(nears[-1]))
    befores = [drives(0, nears[-1]), drives(1, nears[-1]), fars[2]]
    small, _ = close(*held, (fars[0], gram_a[0]), befores, kept_base)
    new_a, new_b, krt = small_step(core, a, b, (*gram_a, *small), news[-1], kept_base, False)

    a, b = new_a, new_b
    lasts, after = [], a
    for place, start, units in LAST:
        near = mass_products(core, krt, parts[place], after, kept_base, start, units)
        after = near
        if not lasts:
            far = over_x(jnp.concatenate([near, a[:rows]], 0))
            far, far_a = far[: units * UNIT], far[units * UNIT :]
        else:
            far = over_x(near)
        lasts.append((2 * place + start, near, far))
    for place in places[2:]:
        drives(place, after)
    total = add(core, sums[0], over_core(sums[1]), (news[-1],), ())
    drive, gram_c = total[: rows + scans], total[rows + scans :]
    drive = drive + swap(drive, "mz", mz, 1)
    gram_a = grams(a, far_a, drive, ())
    base, scale = mass_base(core, *gram_a, b, news, drive, ())
    stages = [[], [], []]
    for i in range(1, mz.bit_length() - 1):
        drive = drive + swap(drive, "mz", mz, 1 << i)
        stages[min(i, 2) - 1].append(drive)
    for i, distance in enumerate([mz >> 1] + [1 << i for i in range(mz.bit_length() - 2)]):
        gram_c = gram_c + swap(gram_c, "mz", mz, distance)
        stages[min(i, 2)].append(gram_c)
    drive, drive_b = drive[:rows], drive[rows:]
    small = gram_c, over_core(gram_c), drive, over_core(drive), drive_b, over_x(drive_b)
    stages[2] += small
    afters = [(scale,)] + stages
    mines = []
    out = None
    for place, (start, near, far) in enumerate(lasts):
        after = tuple(afters[place]) if place < len(afters) else ()
        if place > 1:
            after += (mark,)
        mine = last_step(core, scale, base, near, far, after, start)
        mines.append((mine, over_core(mine)))
        if place:
            out, mark = join(core, *mines[place - 1], out, mine, place - 1, bins)
    new_a, new_b = small_step(core, a, b, (*gram_a, *small), mines[-1][0], (), True)
    out, mark = join(core, *mines[-1], out, new_b, len(lasts) - 1, bins)
    return new_a, new_b, out


def solution(mesh):
    placed = (P("grp", None, "mz"), P("grp", None), P(), P("mz", None))
    return jax.shard_map(
        functools.partial(local, mesh.shape["mz"]),
        mesh=mesh,
        in_specs=placed,
        out_specs=(P("grp", None), P(), P("mz", None)),
        check_vma=False,
    )
```

```python
import functools

import jax
import jax.numpy as jnp
from jax import lax
from jax.experimental import pallas as pl
from jax.experimental.pallas import tpu as pltpu
from jax.sharding import PartitionSpec as P

STEPS = 2
UNIT = 256
PAIR = 2 * UNIT
FIRST = (False, True, True, False)
LAST = ((0, 0, 2), (1, 0, 2), (2, 0, 2), (3, 0, 2))
F32 = jnp.float32
BF16 = jnp.bfloat16
VMEM_LIMIT = 6 << 20
LOAD_VMEM_LIMIT = 20 << 20
NOWHERE = pl.BlockSpec(memory_space=pl.ANY)
HELD = pl.BlockSpec(memory_space=pltpu.VMEM)


def split(value):
    high = value.astype(BF16)
    return high, (value - high.astype(F32)).astype(BF16)


def plain(a, b):
    return jnp.dot(a, b, preferred_element_type=F32)


def dot(a, b):
    a_high, a_low = split(a)
    b_high, b_low = split(b)
    return plain(a_high, b_high) + (plain(a_high, b_low) + plain(a_low, b_high))


def gram(factor):
    return dot(factor.T, factor)


def inverse_norm(matrix):
    return 1.0 / jnp.sqrt(jnp.sum(matrix * matrix, keepdims=True) + 1e-12)


def in_vmem(value):
    return pltpu.with_memory_space_constraint(value, pltpu.VMEM)


def shaped(*dims):
    return jax.ShapeDtypeStruct(dims, F32)


def whole(shape):
    return pl.BlockSpec(shape, lambda *_: (0,) * len(shape))


def in_hbm(value):
    return pltpu.with_memory_space_constraint(value, pltpu.HBM)


def rows_block(rows, rank, start=0):
    return pl.BlockSpec((rows, rank), lambda j, *_: (start + j, 0))


def call(kernel, name, grid, in_specs, out_specs, out_shape, scratch=(), aliases=None, kept=()):
    inputs = len(in_specs)

    def without_kept(core_ref, *refs):
        kernel(core_ref, *refs[:inputs], *refs[inputs + len(kept) :])

    run = pl.pallas_call(
        without_kept if kept else kernel,
        grid_spec=pltpu.PrefetchScalarGridSpec(
            num_scalar_prefetch=1,
            grid=grid,
            in_specs=list(in_specs) + [HELD for _ in kept],
            out_specs=out_specs,
            scratch_shapes=scratch,
        ),
        out_shape=out_shape,
        input_output_aliases=aliases or {},
        cost_estimate=pl.CostEstimate(flops=0, bytes_accessed=0, transcendentals=0),
        compiler_params=pltpu.CompilerParams(
            vmem_limit_bytes=LOAD_VMEM_LIMIT if name in ("load", "first_products") else VMEM_LIMIT
        ),
        name=name,
    )
    return lambda *args: run(*args, *(in_vmem(value) for value in kept))


def give_kernel(start, core_ref, x_ref, after_ref, out_ref, sem):
    bins = x_ref.shape[1]
    column = (1 - core_ref[0]) * (bins // 2) + start * PAIR
    copy = pltpu.make_async_copy(
        x_ref.at[:, pl.ds(pl.multiple_of(column, PAIR), PAIR)], out_ref, sem
    )
    copy.start()
    copy.wait()


def give(core, x, after, start):
    return call(
        functools.partial(give_kernel, start),
        "give",
        (1,),
        [NOWHERE, NOWHERE],
        HELD,
        pltpu.VMEM((x.shape[0], PAIR), F32),
        [pltpu.SemaphoreType.DMA],
    )(core, in_hbm(x), after)


def add_kernel(core_ref, near_ref, far_ref, *refs):
    refs[-1][...] = near_ref[...] + far_ref[...]


def add(core, near, far, after, kept):
    block = whole(near.shape)
    return call(
        add_kernel,
        "add",
        (1,),
        [block, block] + [NOWHERE for _ in after],
        block,
        shaped(*near.shape),
        kept=kept,
    )(core, near, far, *after)


def fill_khatri_rao(krt_ref, a, b):
    rank = a.shape[1]
    product = (a[:, None, :] * b[None, :, :]).reshape(-1, rank).T
    krt_ref[:rank], krt_ref[rank:] = split(product)


def mass_part(krt_ref, x_high, x_low):
    rank = krt_ref.shape[0] // 2
    both = plain(krt_ref[...], x_high)
    return (both[:rank] + (both[rank:] + plain(krt_ref[:rank], x_low))).T


def contract(x_high, x_low, c):
    rank = c.shape[1]
    c_high, c_low = split(c)
    both = plain(x_high, jnp.concatenate([c_high, c_low], 1))
    return both[:, :rank] + (both[:, rank:] + plain(x_low, c_high))


def store_sums(core, keep_ref, send_ref, total, squares, a, b):
    both = a.shape[0]
    rows, scans, half = both // 2, b.shape[0], squares.shape[0] // 2
    folded = total.reshape(both, scans, a.shape[1])
    drive = jnp.sum(folded * b[None], 1)
    drive_b = jnp.sum(folded * a[:, None, :], 0)
    keep_ref[:rows], send_ref[:rows] = drive[:rows], drive[rows:]
    keep_ref[rows : rows + scans] = drive_b
    send_ref[rows : rows + scans] = drive_b
    at_zero = core == 0
    keep_ref[rows + scans :] = jnp.where(at_zero, squares[:half], squares[half:])
    send_ref[rows + scans :] = jnp.where(at_zero, squares[half:], squares[:half])


def load_kernel(started, last, with_mass, core_ref, a_ref, b_ref, x_ref, other_ref, c_ref, krt_in_ref, total_in_ref, gram_in_ref, after_ref, *refs):
    high_ref, low_ref, *refs = refs
    if with_mass:
        mass_ref, *refs = refs
    if last:
        keep_ref, send_ref, *refs = refs
    total_ref, gram_ref, *refs = refs
    krt_ref = krt_in_ref if started else refs[0]
    step = pl.program_id(0)
    rows = x_ref.shape[0]

    @pl.when(step == 0)
    def _():
        total_ref[...] = total_in_ref[...] if started else jnp.zeros_like(total_ref)
        gram_ref[...] = gram_in_ref[...] if started else jnp.zeros_like(gram_ref)
        if not started:
            fill_khatri_rao(krt_ref, a_ref[...], b_ref[...])

    high_ref[step, :rows], low_ref[step, :rows] = split(x_ref[...])
    high_ref[step, rows:], low_ref[step, rows:] = split(other_ref[...])
    x_high, x_low = high_ref[step], low_ref[step]
    if with_mass:
        mass_ref[...] = mass_part(krt_ref, x_high, x_low)
    c = c_ref[...]
    total_ref[...] += contract(x_high, x_low, c)
    gram_ref[...] += gram(c)

    if last:

        @pl.when(step == pl.num_programs(0) - 1)
        def _():
            store_sums(
                core_ref[0], keep_ref, send_ref, total_ref[...], gram_ref[...], a_ref[...], b_ref[...]
            )


def load(core, a, b, x, other, c, krt, held, after, kept, start, last, with_mass):
    rows, bins = x.shape
    rank = c.shape[1]
    blocks = bins // (2 * PAIR)
    started = held is not None
    units = other.shape[1] // PAIR
    part = pltpu.VMEM((units, 2 * rows, PAIR), BF16)
    mass = [shaped(units * PAIR, rank)] if with_mass else []
    total, squares = shaped(2 * rows, rank), shaped(rank, rank)
    sums = shaped(a.shape[0] // 2 + b.shape[0] + rank // 2, rank)
    tail = [sums, sums] if last else [pltpu.VMEM(total.shape, F32), squares]
    tail_specs = [whole(sums.shape)] * 2 if last else [HELD, whole(squares.shape)]
    if not started:
        tail.append(pltpu.VMEM((2 * rank, 2 * rows), BF16))
        tail_specs.append(HELD)
    return call(
        functools.partial(load_kernel, started, last, with_mass),
        "load",
        (units,),
        [
            whole(a.shape),
            whole(b.shape),
            pl.BlockSpec((rows, PAIR), lambda j, core_ref: (0, core_ref[0] * blocks + start + j)),
            pl.BlockSpec((rows, PAIR), lambda j, core_ref: (0, j)),
            pl.BlockSpec((PAIR, rank), lambda j, core_ref: (core_ref[0] * blocks + start + j, 0)),
            HELD if started else NOWHERE,
            HELD if started else NOWHERE,
            whole(squares.shape) if started else NOWHERE,
            NOWHERE,
        ],
        [HELD, HELD] + [rows_block(PAIR, rank) for _ in mass] + tail_specs,
        [part, part] + mass + tail,
        [pltpu.VMEM(total.shape, F32), pltpu.VMEM(squares.shape, F32)] if last else [],
        kept=kept,
    )(
        core,
        a,
        b,
        in_hbm(x),
        in_hbm(other) if not started else other,
        in_hbm(c),
        in_vmem(krt) if started else after,
        in_vmem(held[0]) if started else after,
        held[1] if started else after,
        after,
    )


def first_kernel(start, core_ref, a_ref, b_ref, x_ref, other_ref, source_ref, after_ref, out_ref, *refs):
    *given, krt_ref, sems = refs
    bins = source_ref.shape[1]
    copies = []
    for place, given_ref in enumerate(given):
        column = (1 - core_ref[0]) * (bins // 2) + (start + place) * PAIR
        columns = pl.ds(pl.multiple_of(column, PAIR), PAIR)
        copies.append(
            pltpu.make_async_copy(source_ref.at[:, columns], given_ref, sems.at[place])
        )
    for copy in copies:
        copy.start()
    fill_khatri_rao(krt_ref, a_ref[...], b_ref[...])
    x_high, x_low = split(jnp.concatenate([x_ref[...], other_ref[...]], 0))
    out_ref[...] = mass_part(krt_ref, x_high, x_low)
    for copy in copies:
        copy.wait()


def first_products(core, a, b, x, other, after, start):
    rows, bins = x.shape
    rank = a.shape[1]
    blocks = bins // (2 * PAIR)
    given = len(FIRST) - start
    return call(
        functools.partial(first_kernel, start),
        "first_products",
        (1,),
        [
            whole(a.shape),
            whole(b.shape),
            pl.BlockSpec((rows, PAIR), lambda j, core_ref: (0, core_ref[0] * blocks)),
            whole(other.shape),
            NOWHERE,
            NOWHERE,
        ],
        [whole((PAIR, rank))] + [HELD] * given,
        [shaped(PAIR, rank)] + [pltpu.VMEM((rows, PAIR), F32)] * given,
        [pltpu.VMEM((2 * rank, 2 * rows), BF16), pltpu.SemaphoreType.DMA((given,))],
    )(core, a, b, in_hbm(x), other, in_hbm(x), after)


def mass_kernel(start, core_ref, krt_ref, high_ref, low_ref, after_ref, out_ref):
    unit = start + pl.program_id(0)
    columns = pl.ds(pl.multiple_of(unit % 2 * UNIT, UNIT), UNIT)
    out_ref[...] = mass_part(krt_ref, high_ref[unit // 2, :, columns], low_ref[unit // 2, :, columns])


def mass_products(core, krt, parts, after, kept, start, units):
    rank = krt.shape[0] // 2
    return call(
        functools.partial(mass_kernel, start),
        "mass_products",
        (units,),
        [HELD, HELD, HELD, NOWHERE],
        rows_block(UNIT, rank),
        shaped(units * UNIT, rank),
        kept=kept,
    )(core, in_vmem(krt), in_vmem(parts[0]), in_vmem(parts[1]), after)


def drive_kernel(start, started, last, core_ref, a_ref, b_ref, scale_ref, high_ref, low_ref, base_ref, near_ref, far_ref, total_in_ref, gram_in_ref, after_ref, *refs):
    if last:
        new_ref, keep_ref, send_ref, total_ref, gram_ref = refs
    else:
        new_ref, total_ref, gram_ref = refs
    step = pl.program_id(0)

    @pl.when(step == 0)
    def _():
        total_ref[...] = total_in_ref[...] if started else jnp.zeros_like(total_ref)
        gram_ref[...] = gram_in_ref[...] if started else jnp.zeros_like(gram_ref)

    place = pl.ds(pl.multiple_of((start + step) * PAIR, PAIR), PAIR)
    new = base_ref[place] + (near_ref[...] + far_ref[...]) * scale_ref[:1, :1]
    new_ref[pl.ds(pl.multiple_of(step * PAIR, PAIR), PAIR)] = new
    total_ref[...] += contract(high_ref[step], low_ref[step], new)
    gram_ref[...] += gram(new)

    if last:

        @pl.when(step == pl.num_programs(0) - 1)
        def _():
            store_sums(
                core_ref[0], keep_ref, send_ref, total_ref[...], gram_ref[...], a_ref[...], b_ref[...]
            )


def drive_products(core, a, b, scale, parts, base, near, far, held, after, kept, start, last):
    rank = a.shape[1]
    units, rows = parts[0].shape[:2]
    started = held is not None
    total, squares = shaped(rows, rank), shaped(rank, rank)
    sums = shaped(a.shape[0] // 2 + b.shape[0] + rank // 2, rank)
    tail = [sums, sums] if last else [pltpu.VMEM(total.shape, F32), squares]
    tail_specs = [whole(sums.shape)] * 2 if last else [HELD, whole(squares.shape)]
    return call(
        functools.partial(drive_kernel, start, started, last),
        "drive_products",
        (units,),
        [
            whole(a.shape),
            whole(b.shape),
            whole(scale.shape),
            HELD,
            HELD,
            HELD,
            rows_block(PAIR, rank),
            rows_block(PAIR, rank),
            HELD if started else NOWHERE,
            whole(squares.shape) if started else NOWHERE,
            NOWHERE,
        ],
        [HELD] + tail_specs,
        [pltpu.VMEM((units * PAIR, rank), F32)] + tail,
        [pltpu.VMEM(total.shape, F32), pltpu.VMEM(squares.shape, F32)] if last else [],
        kept=kept,
    )(
        core,
        a,
        b,
        scale,
        in_vmem(parts[0]),
        in_vmem(parts[1]),
        in_vmem(base),
        near,
        far,
        in_vmem(held[0]) if started else after,
        held[1] if started else after,
        after,
    )


def base_kernel(core_ref, gram_ref, other_ref, b_ref, after_ref, *refs):
    out_ref, scale_ref = refs[-2:]
    hessian = (gram_ref[...] + other_ref[...]) * gram(b_ref[...])
    scale = inverse_norm(hessian)
    hessian = hessian * scale
    scale_ref[...] = jnp.broadcast_to(scale, scale_ref.shape)
    done = 0
    for c_ref in refs[:-2]:
        for start in range(0, c_ref.shape[0], PAIR):
            c = c_ref[start : start + PAIR]
            out_ref[done : done + PAIR] = c - dot(c, hessian)
            done += PAIR


def mass_base(core, gram_a, gram_a_other, b, pieces, after, kept):
    rank = b.shape[1]
    square = whole((rank, rank))
    scale = shaped(8, rank)
    bins = sum(piece.shape[0] for piece in pieces)
    return call(
        base_kernel,
        "mass_base",
        (1,),
        [square, square, whole(b.shape), NOWHERE] + [HELD for _ in pieces],
        [HELD, whole(scale.shape)],
        (pltpu.VMEM((bins, rank), F32), scale),
        kept=kept,
    )(core, gram_a, gram_a_other, b, after, *(in_vmem(piece) for piece in pieces))


def last_kernel(start, core_ref, scale_ref, base_ref, near_ref, far_ref, *refs):
    place = pl.ds(pl.multiple_of((start + pl.program_id(0)) * UNIT, UNIT), UNIT)
    refs[-1][...] = base_ref[place] + (near_ref[...] + far_ref[...]) * scale_ref[:1, :1]


def last_step(core, scale, base, near, far, after, start):
    rank = base.shape[1]
    side = rows_block(UNIT, rank)
    return call(
        functools.partial(last_kernel, start),
        "last_step",
        (near.shape[0] // UNIT,),
        [whole(scale.shape), HELD, side, side] + [NOWHERE for _ in after],
        side,
        shaped(*near.shape),
    )(core, scale, in_vmem(base), near, far, *after)


def join_kernel(core_ref, mine_ref, theirs_ref, held_ref, after_ref, out_ref, done_ref):
    done_ref[...] = jnp.zeros_like(done_ref)

    @pl.when(pl.program_id(0) == 0)
    def _():
        out_ref[...] = mine_ref[...]

    @pl.when(pl.program_id(0) == 1)
    def _():
        out_ref[...] = theirs_ref[...]


def join(core, mine, theirs, held, after, chunk, bins):
    rows, rank = mine.shape
    chunks = bins // (2 * rows)
    first = held is None

    def place(side, core_ref):
        return jnp.where(side == 0, core_ref[0], 1 - core_ref[0]) * chunks + chunk, 0

    return call(
        join_kernel,
        "join",
        (2,),
        [whole(mine.shape), whole(mine.shape), NOWHERE, NOWHERE],
        [pl.BlockSpec((rows, rank), place), whole((8, 128))],
        (shaped(bins, rank), shaped(8, 128)),
        (),
        {} if first else {3: 0},
    )(core, mine, theirs, mine if first else held, after)


def sample_gram_kernel(core_ref, a_ref, far_ref, after_ref, out_ref):
    out_ref[...] = gram(a_ref[...]) + gram(far_ref[...])


def sample_gram(core, a, far, after, kept):
    rank = a.shape[1]
    return call(
        sample_gram_kernel,
        "sample_gram",
        (1,),
        [whole(a.shape), whole(a.shape), NOWHERE],
        whole((rank, rank)),
        shaped(rank, rank),
        kept=kept,
    )(core, a, far, after)


def small_step_kernel(
    core_ref,
    a_ref,
    b_ref,
    gram_a_ref,
    gram_a_other_ref,
    gram_c_ref,
    gram_c_other_ref,
    drive_ref,
    drive_other_ref,
    drive_b_ref,
    drive_b_far_ref,
    after_ref,
    new_a_ref,
    new_b_ref,
    *refs,
):
    a, b = a_ref[...], b_ref[...]
    gram_a = gram_a_ref[...] + gram_a_other_ref[...]
    at_zero = core_ref[0] == 0
    mine, other = gram_c_ref[...], gram_c_other_ref[...]
    gram_c = jnp.concatenate([jnp.where(at_zero, mine, other), jnp.where(at_zero, other, mine)], 0)
    hessian_a = gram(b) * gram_c
    hessian_b = gram_a * gram_c
    drive_a = jnp.concatenate([drive_ref[...], drive_other_ref[...]], 0)
    drive_b = drive_b_ref[...] + drive_b_far_ref[...]
    new_a = a - (dot(a, hessian_a) - drive_a) * inverse_norm(hessian_a)
    new_b = b - (dot(b, hessian_b) - drive_b) * inverse_norm(hessian_b)
    new_a_ref[...] = new_a[: new_a_ref.shape[0]]
    new_b_ref[...] = new_b
    if refs:
        fill_khatri_rao(refs[0], new_a, new_b)


def small_step(core, a, b, args, after, kept, last):
    rows = a.shape[0] // 2 if last else a.shape[0]
    outs = [shaped(rows, a.shape[1]), shaped(*b.shape)]
    specs = [whole(outs[0].shape), whole(b.shape)]
    if not last:
        outs.append(pltpu.VMEM((2 * a.shape[1], a.shape[0] * b.shape[0]), BF16))
        specs.append(HELD)
    return call(
        small_step_kernel,
        "small_step",
        (1,),
        [whole(v.shape) for v in (a, b, *args)] + [NOWHERE],
        specs,
        outs,
        kept=kept,
    )(core, a, b, *args, after)


def swap(value, axis, size, distance):
    return lax.ppermute(value, axis, [(i, i ^ distance) for i in range(size)])


def local(mz, intensities, sample_start, scan_start, mass_start):
    b, c = scan_start, mass_start
    bins, rank = c.shape
    rows, scans = sample_start.shape[0], b.shape[0]
    x = intensities.reshape(-1, bins)
    number = lax.axis_index("grp") % 2
    core = number.reshape(1).astype(jnp.int32)

    def over_core(value):
        return swap(value, "grp", 4, 1)

    def over_x(value):
        return swap(value, "grp", 4, 2)

    def sum_mz(value, first, befores, kept, done=0):
        values = []
        distances = [1 << i for i in range(mz.bit_length() - 1)]
        place = distances.index(first)
        for distance in (distances[place:] + distances[:place])[: len(distances) - done]:
            far = swap(value, "mz", mz, distance)
            after, *befores = befores or [None]
            value = value + far if after is None else add(core, value, far, (after,), kept)
            values.append(value)
        return value, values[0]

    def close(keep, send, before, befores, kept):
        total = add(core, keep, over_core(send), before, kept)
        gram_c, _ = sum_mz(total[rows + scans :], mz // 2, [], kept)
        drive, early = sum_mz(total[: rows + scans], 1, befores, kept)
        drive, drive_b = drive[:rows], drive[rows:]
        return (gram_c, over_core(gram_c), drive, over_core(drive), drive_b, over_x(drive_b)), early

    def grams(a, far, after, kept):
        part = sample_gram(core, a[:rows], far, after, kept)
        return part, over_core(part)

    places = range(len(FIRST))
    others, after = [], x
    for place in places[:2]:
        after = give(core, x, after, place)
        others.append(over_core(after))
    a = jnp.concatenate([sample_start, over_core(sample_start)], 0)
    far_a = over_x(sample_start)

    near, *given = first_products(core, a, b, x, others[0], after, len(others))
    others += [over_core(value) for value in given]
    parts, nears = [], [near]
    kept = ()
    after = near
    krt, held = None, None
    for place in places:
        high, low, *rest = load(
            core, a, b, x, others[place], c, krt, held, after, kept, place, place == places[-1], FIRST[place]
        )
        if FIRST[place]:
            after, *rest = rest
            nears.append(after)
        if krt is None:
            krt = rest.pop()
        held = rest
        parts.append((high, low))
        kept += (high, low)
        if place == places[-1]:
            gram_a = grams(a, far_a, held[0], kept)
            c_mine = lax.dynamic_slice_in_dim(c, number * (bins // 2), bins // 2, 0)
            base, scale = mass_base(core, *gram_a, b, [c_mine], after, kept)

    fars = [over_x(near) for near in nears]
    news, sums = [], None
    kept_base = kept + (base,)

    def drives(place, after):
        nonlocal sums
        new, *sums = drive_products(
            core,
            a,
            b,
            scale,
            parts[place],
            base,
            nears[place],
            fars[place],
            sums,
            after,
            kept,
            place,
            place == places[-1],
        )
        news.append(new)
        return new

    old_a = a
    after = held[0]
    for place in places[len(nears) :]:
        after = mass_products(core, krt, parts[place], after, kept_base, 0, 2)
        nears.append(after)
        fars.append(over_x(nears[-1]))
    befores = [drives(0, nears[-1]), drives(1, nears[-1]), fars[2]]
    small, _ = close(*held, (fars[0], gram_a[0]), befores, kept_base)
    new_a, new_b, krt = small_step(core, a, b, (*gram_a, *small), news[-1], kept_base, False)

    a, b = new_a, new_b
    lasts, after = [], a
    for place, start, units in LAST:
        near = mass_products(core, krt, parts[place], after, kept_base, start, units)
        after = near
        if not lasts:
            far = over_x(jnp.concatenate([near, a[:rows]], 0))
            far, far_a = far[: units * UNIT], far[units * UNIT :]
        else:
            far = over_x(near)
        lasts.append((2 * place + start, near, far))
    for place in places[2:]:
        drives(place, after)
    total = add(core, sums[0], over_core(sums[1]), (news[-1],), ())
    drive, gram_c = total[: rows + scans], total[rows + scans :]
    drive = drive + swap(drive, "mz", mz, 1)
    gram_a = grams(a, far_a, drive, ())
    base, scale = mass_base(core, *gram_a, b, news, drive, ())
    stages = [[], [], []]
    for i in range(1, mz.bit_length() - 1):
        drive = drive + swap(drive, "mz", mz, 1 << i)
        stages[min(i, 2) - 1].append(drive)
    for i, distance in enumerate([mz >> 1] + [1 << i for i in range(mz.bit_length() - 2)]):
        gram_c = gram_c + swap(gram_c, "mz", mz, distance)
        stages[min(i, 2)].append(gram_c)
    drive, drive_b = drive[:rows], drive[rows:]
    small = gram_c, over_core(gram_c), drive, over_core(drive), drive_b, over_x(drive_b)
    stages[2] += small
    afters = [(scale,)] + stages
    mines = []
    out = None
    for place, (start, near, far) in enumerate(lasts):
        after = tuple(afters[place]) if place < len(afters) else ()
        if place > 1:
            after += (mark,)
        mine = last_step(core, scale, base, near, far, after, start)
        mines.append((mine, over_core(mine)))
        if place:
            out, mark = join(core, *mines[place - 1], out, mine, place - 1, bins)
    new_a, new_b = small_step(core, a, b, (*gram_a, *small), mines[-1][0], (), True)
    out, mark = join(core, *mines[-1], out, new_b, len(lasts) - 1, bins)
    return new_a, new_b, out


def solution(mesh):
    placed = (P("grp", None, "mz"), P("grp", None), P(), P("mz", None))
    return jax.shard_map(
        functools.partial(local, mesh.shape["mz"]),
        mesh=mesh,
        in_specs=placed,
        out_specs=(P("grp", None), P(), P("mz", None)),
        check_vma=False,
    )
```

```python
import functools

import jax
import jax.numpy as jnp
from jax import lax
from jax.experimental import pallas as pl
from jax.experimental.pallas import tpu as pltpu
from jax.sharding import PartitionSpec as P

STEPS = 2
UNIT = 256
PAIR = 2 * UNIT
FIRST = (False, True, True, False)
LAST = ((0, 0, 2), (1, 0, 2), (2, 0, 2), (3, 0, 2))
F32 = jnp.float32
BF16 = jnp.bfloat16
VMEM_LIMIT = 6 << 20
LOAD_VMEM_LIMIT = 20 << 20
NOWHERE = pl.BlockSpec(memory_space=pl.ANY)
HELD = pl.BlockSpec(memory_space=pltpu.VMEM)


def split(value):
    high = value.astype(BF16)
    return high, (value - high.astype(F32)).astype(BF16)


def plain(a, b):
    return jnp.dot(a, b, preferred_element_type=F32)


def dot(a, b):
    a_high, a_low = split(a)
    b_high, b_low = split(b)
    return plain(a_high, b_high) + (plain(a_high, b_low) + plain(a_low, b_high))


def gram(factor):
    return dot(factor.T, factor)


def inverse_norm(matrix):
    return 1.0 / jnp.sqrt(jnp.sum(matrix * matrix, keepdims=True) + 1e-12)


def in_vmem(value):
    return pltpu.with_memory_space_constraint(value, pltpu.VMEM)


def shaped(*dims):
    return jax.ShapeDtypeStruct(dims, F32)


def whole(shape):
    return pl.BlockSpec(shape, lambda *_: (0,) * len(shape))


def in_hbm(value):
    return pltpu.with_memory_space_constraint(value, pltpu.HBM)


def rows_block(rows, rank, start=0):
    return pl.BlockSpec((rows, rank), lambda j, *_: (start + j, 0))


def call(kernel, name, grid, in_specs, out_specs, out_shape, scratch=(), aliases=None, kept=()):
    inputs = len(in_specs)

    def without_kept(core_ref, *refs):
        kernel(core_ref, *refs[:inputs], *refs[inputs + len(kept) :])

    run = pl.pallas_call(
        without_kept if kept else kernel,
        grid_spec=pltpu.PrefetchScalarGridSpec(
            num_scalar_prefetch=1,
            grid=grid,
            in_specs=list(in_specs) + [HELD for _ in kept],
            out_specs=out_specs,
            scratch_shapes=scratch,
        ),
        out_shape=out_shape,
        input_output_aliases=aliases or {},
        cost_estimate=pl.CostEstimate(flops=0, bytes_accessed=0, transcendentals=0),
        compiler_params=pltpu.CompilerParams(
            vmem_limit_bytes=LOAD_VMEM_LIMIT if name in ("load", "first_products") else VMEM_LIMIT
        ),
        name=name,
    )
    return lambda *args: run(*args, *(in_vmem(value) for value in kept))


def give_kernel(start, core_ref, x_ref, after_ref, out_ref, sem):
    bins = x_ref.shape[1]
    column = (1 - core_ref[0]) * (bins // 2) + start * PAIR
    copy = pltpu.make_async_copy(
        x_ref.at[:, pl.ds(pl.multiple_of(column, PAIR), PAIR)], out_ref, sem
    )
    copy.start()
    copy.wait()


def give(core, x, after, start):
    return call(
        functools.partial(give_kernel, start),
        "give",
        (1,),
        [NOWHERE, NOWHERE],
        HELD,
        pltpu.VMEM((x.shape[0], PAIR), F32),
        [pltpu.SemaphoreType.DMA],
    )(core, in_hbm(x), after)


def add_kernel(core_ref, near_ref, far_ref, *refs):
    refs[-1][...] = near_ref[...] + far_ref[...]


def add(core, near, far, after, kept):
    block = whole(near.shape)
    return call(
        add_kernel,
        "add",
        (1,),
        [block, block] + [NOWHERE for _ in after],
        block,
        shaped(*near.shape),
        kept=kept,
    )(core, near, far, *after)


def fill_khatri_rao(krt_ref, a, b):
    rank = a.shape[1]
    product = (a[:, None, :] * b[None, :, :]).reshape(-1, rank).T
    krt_ref[:rank], krt_ref[rank:] = split(product)


def mass_part(krt_ref, x_high, x_low):
    rank = krt_ref.shape[0] // 2
    both = plain(krt_ref[...], x_high)
    return (both[:rank] + (both[rank:] + plain(krt_ref[:rank], x_low))).T


def contract(x_high, x_low, c):
    rank = c.shape[1]
    c_high, c_low = split(c)
    both = plain(x_high, jnp.concatenate([c_high, c_low], 1))
    return both[:, :rank] + (both[:, rank:] + plain(x_low, c_high))


def store_sums(core, keep_ref, send_ref, total, squares, a, b):
    both = a.shape[0]
    rows, scans, half = both // 2, b.shape[0], squares.shape[0] // 2
    folded = total.reshape(both, scans, a.shape[1])
    drive = jnp.sum(folded * b[None], 1)
    drive_b = jnp.sum(folded * a[:, None, :], 0)
    keep_ref[:rows], send_ref[:rows] = drive[:rows], drive[rows:]
    keep_ref[rows : rows + scans] = drive_b
    send_ref[rows : rows + scans] = drive_b
    at_zero = core == 0
    keep_ref[rows + scans :] = jnp.where(at_zero, squares[:half], squares[half:])
    send_ref[rows + scans :] = jnp.where(at_zero, squares[half:], squares[:half])


def load_kernel(started, last, with_mass, core_ref, a_ref, b_ref, x_ref, other_ref, c_ref, krt_in_ref, total_in_ref, gram_in_ref, after_ref, *refs):
    high_ref, low_ref, *refs = refs
    if with_mass:
        mass_ref, *refs = refs
    if last:
        keep_ref, send_ref, *refs = refs
    total_ref, gram_ref, *refs = refs
    krt_ref = krt_in_ref if started else refs[0]
    step = pl.program_id(0)
    rows = x_ref.shape[0]

    @pl.when(step == 0)
    def _():
        total_ref[...] = total_in_ref[...] if started else jnp.zeros_like(total_ref)
        gram_ref[...] = gram_in_ref[...] if started else jnp.zeros_like(gram_ref)
        if not started:
            fill_khatri_rao(krt_ref, a_ref[...], b_ref[...])

    high_ref[step, :rows], low_ref[step, :rows] = split(x_ref[...])
    high_ref[step, rows:], low_ref[step, rows:] = split(other_ref[...])
    x_high, x_low = high_ref[step], low_ref[step]
    if with_mass:
        mass_ref[...] = mass_part(krt_ref, x_high, x_low)
    c = c_ref[...]
    total_ref[...] += contract(x_high, x_low, c)
    gram_ref[...] += gram(c)

    if last:

        @pl.when(step == pl.num_programs(0) - 1)
        def _():
            store_sums(
                core_ref[0], keep_ref, send_ref, total_ref[...], gram_ref[...], a_ref[...], b_ref[...]
            )


def load(core, a, b, x, other, c, krt, held, after, kept, start, last, with_mass):
    rows, bins = x.shape
    rank = c.shape[1]
    blocks = bins // (2 * PAIR)
    started = held is not None
    units = other.shape[1] // PAIR
    part = pltpu.VMEM((units, 2 * rows, PAIR), BF16)
    mass = [shaped(units * PAIR, rank)] if with_mass else []
    total, squares = shaped(2 * rows, rank), shaped(rank, rank)
    sums = shaped(a.shape[0] // 2 + b.shape[0] + rank // 2, rank)
    tail = [sums, sums] if last else [pltpu.VMEM(total.shape, F32), squares]
    tail_specs = [whole(sums.shape)] * 2 if last else [HELD, whole(squares.shape)]
    if not started:
        tail.append(pltpu.VMEM((2 * rank, 2 * rows), BF16))
        tail_specs.append(HELD)
    return call(
        functools.partial(load_kernel, started, last, with_mass),
        "load",
        (units,),
        [
            whole(a.shape),
            whole(b.shape),
            pl.BlockSpec((rows, PAIR), lambda j, core_ref: (0, core_ref[0] * blocks + start + j)),
            pl.BlockSpec((rows, PAIR), lambda j, core_ref: (0, j)),
            pl.BlockSpec((PAIR, rank), lambda j, core_ref: (core_ref[0] * blocks + start + j, 0)),
            HELD if started else NOWHERE,
            HELD if started else NOWHERE,
            whole(squares.shape) if started else NOWHERE,
            NOWHERE,
        ],
        [HELD, HELD] + [rows_block(PAIR, rank) for _ in mass] + tail_specs,
        [part, part] + mass + tail,
        [pltpu.VMEM(total.shape, F32), pltpu.VMEM(squares.shape, F32)] if last else [],
        kept=kept,
    )(
        core,
        a,
        b,
        in_hbm(x),
        in_hbm(other) if not started else other,
        in_hbm(c),
        in_vmem(krt) if started else after,
        in_vmem(held[0]) if started else after,
        held[1] if started else after,
        after,
    )


def first_kernel(start, core_ref, a_ref, b_ref, x_ref, other_ref, source_ref, after_ref, out_ref, *refs):
    *given, krt_ref, sems = refs
    bins = source_ref.shape[1]
    copies = []
    for place, given_ref in enumerate(given):
        column = (1 - core_ref[0]) * (bins // 2) + (start + place) * PAIR
        columns = pl.ds(pl.multiple_of(column, PAIR), PAIR)
        copies.append(
            pltpu.make_async_copy(source_ref.at[:, columns], given_ref, sems.at[place])
        )
    for copy in copies:
        copy.start()
    fill_khatri_rao(krt_ref, a_ref[...], b_ref[...])
    x_high, x_low = split(jnp.concatenate([x_ref[...], other_ref[...]], 0))
    out_ref[...] = mass_part(krt_ref, x_high, x_low)
    for copy in copies:
        copy.wait()


def first_products(core, a, b, x, other, after, start):
    rows, bins = x.shape
    rank = a.shape[1]
    blocks = bins // (2 * PAIR)
    given = len(FIRST) - start
    return call(
        functools.partial(first_kernel, start),
        "first_products",
        (1,),
        [
            whole(a.shape),
            whole(b.shape),
            pl.BlockSpec((rows, PAIR), lambda j, core_ref: (0, core_ref[0] * blocks)),
            whole(other.shape),
            NOWHERE,
            NOWHERE,
        ],
        [whole((PAIR, rank))] + [HELD] * given,
        [shaped(PAIR, rank)] + [pltpu.VMEM((rows, PAIR), F32)] * given,
        [pltpu.VMEM((2 * rank, 2 * rows), BF16), pltpu.SemaphoreType.DMA((given,))],
    )(core, a, b, in_hbm(x), other, in_hbm(x), after)


def mass_kernel(start, core_ref, krt_ref, high_ref, low_ref, after_ref, out_ref):
    unit = start + pl.program_id(0)
    columns = pl.ds(pl.multiple_of(unit % 2 * UNIT, UNIT), UNIT)
    out_ref[...] = mass_part(krt_ref, high_ref[unit // 2, :, columns], low_ref[unit // 2, :, columns])


def mass_products(core, krt, parts, after, kept, start, units):
    rank = krt.shape[0] // 2
    return call(
        functools.partial(mass_kernel, start),
        "mass_products",
        (units,),
        [HELD, HELD, HELD, NOWHERE],
        rows_block(UNIT, rank),
        shaped(units * UNIT, rank),
        kept=kept,
    )(core, in_vmem(krt), in_vmem(parts[0]), in_vmem(parts[1]), after)


def drive_kernel(start, started, last, core_ref, a_ref, b_ref, scale_ref, high_ref, low_ref, base_ref, near_ref, far_ref, total_in_ref, gram_in_ref, after_ref, *refs):
    if last:
        new_ref, keep_ref, send_ref, total_ref, gram_ref = refs
    else:
        new_ref, total_ref, gram_ref = refs
    step = pl.program_id(0)

    @pl.when(step == 0)
    def _():
        total_ref[...] = total_in_ref[...] if started else jnp.zeros_like(total_ref)
        gram_ref[...] = gram_in_ref[...] if started else jnp.zeros_like(gram_ref)

    place = pl.ds(pl.multiple_of((start + step) * PAIR, PAIR), PAIR)
    new = base_ref[place] + (near_ref[...] + far_ref[...]) * scale_ref[:1, :1]
    new_ref[pl.ds(pl.multiple_of(step * PAIR, PAIR), PAIR)] = new
    total_ref[...] += contract(high_ref[step], low_ref[step], new)
    gram_ref[...] += gram(new)

    if last:

        @pl.when(step == pl.num_programs(0) - 1)
        def _():
            store_sums(
                core_ref[0], keep_ref, send_ref, total_ref[...], gram_ref[...], a_ref[...], b_ref[...]
            )


def drive_products(core, a, b, scale, parts, base, near, far, held, after, kept, start, last):
    rank = a.shape[1]
    units, rows = parts[0].shape[:2]
    started = held is not None
    total, squares = shaped(rows, rank), shaped(rank, rank)
    sums = shaped(a.shape[0] // 2 + b.shape[0] + rank // 2, rank)
    tail = [sums, sums] if last else [pltpu.VMEM(total.shape, F32), squares]
    tail_specs = [whole(sums.shape)] * 2 if last else [HELD, whole(squares.shape)]
    return call(
        functools.partial(drive_kernel, start, started, last),
        "drive_products",
        (units,),
        [
            whole(a.shape),
            whole(b.shape),
            whole(scale.shape),
            HELD,
            HELD,
            HELD,
            rows_block(PAIR, rank),
            rows_block(PAIR, rank),
            HELD if started else NOWHERE,
            whole(squares.shape) if started else NOWHERE,
            NOWHERE,
        ],
        [HELD] + tail_specs,
        [pltpu.VMEM((units * PAIR, rank), F32)] + tail,
        [pltpu.VMEM(total.shape, F32), pltpu.VMEM(squares.shape, F32)] if last else [],
        kept=kept,
    )(
        core,
        a,
        b,
        scale,
        in_vmem(parts[0]),
        in_vmem(parts[1]),
        in_vmem(base),
        near,
        far,
        in_vmem(held[0]) if started else after,
        held[1] if started else after,
        after,
    )


def base_kernel(core_ref, gram_ref, other_ref, b_ref, after_ref, *refs):
    out_ref, scale_ref = refs[-2:]
    hessian = (gram_ref[...] + other_ref[...]) * gram(b_ref[...])
    scale = inverse_norm(hessian)
    hessian = hessian * scale
    scale_ref[...] = jnp.broadcast_to(scale, scale_ref.shape)
    done = 0
    for c_ref in refs[:-2]:
        for start in range(0, c_ref.shape[0], PAIR):
            c = c_ref[start : start + PAIR]
            out_ref[done : done + PAIR] = c - dot(c, hessian)
            done += PAIR


def mass_base(core, gram_a, gram_a_other, b, pieces, after, kept):
    rank = b.shape[1]
    square = whole((rank, rank))
    scale = shaped(8, rank)
    bins = sum(piece.shape[0] for piece in pieces)
    return call(
        base_kernel,
        "mass_base",
        (1,),
        [square, square, whole(b.shape), NOWHERE] + [HELD for _ in pieces],
        [HELD, whole(scale.shape)],
        (pltpu.VMEM((bins, rank), F32), scale),
        kept=kept,
    )(core, gram_a, gram_a_other, b, after, *(in_vmem(piece) for piece in pieces))


def last_kernel(start, core_ref, scale_ref, base_ref, near_ref, far_ref, *refs):
    place = pl.ds(pl.multiple_of((start + pl.program_id(0)) * UNIT, UNIT), UNIT)
    refs[-1][...] = base_ref[place] + (near_ref[...] + far_ref[...]) * scale_ref[:1, :1]


def last_step(core, scale, base, near, far, after, start):
    rank = base.shape[1]
    side = rows_block(UNIT, rank)
    return call(
        functools.partial(last_kernel, start),
        "last_step",
        (near.shape[0] // UNIT,),
        [whole(scale.shape), HELD, side, side] + [NOWHERE for _ in after],
        side,
        shaped(*near.shape),
    )(core, scale, in_vmem(base), near, far, *after)


def join_kernel(core_ref, mine_ref, theirs_ref, held_ref, after_ref, out_ref, done_ref):
    done_ref[...] = jnp.zeros_like(done_ref)

    @pl.when(pl.program_id(0) == 0)
    def _():
        out_ref[...] = mine_ref[...]

    @pl.when(pl.program_id(0) == 1)
    def _():
        out_ref[...] = theirs_ref[...]


def join(core, mine, theirs, held, after, chunk, bins):
    rows, rank = mine.shape
    chunks = bins // (2 * rows)
    first = held is None

    def place(side, core_ref):
        return jnp.where(side == 0, core_ref[0], 1 - core_ref[0]) * chunks + chunk, 0

    return call(
        join_kernel,
        "join",
        (2,),
        [whole(mine.shape), whole(mine.shape), NOWHERE, NOWHERE],
        [pl.BlockSpec((rows, rank), place), whole((8, 128))],
        (shaped(bins, rank), shaped(8, 128)),
        (),
        {} if first else {3: 0},
    )(core, mine, theirs, mine if first else held, after)


def sample_gram_kernel(core_ref, a_ref, far_ref, after_ref, out_ref):
    out_ref[...] = gram(a_ref[...]) + gram(far_ref[...])


def sample_gram(core, a, far, after, kept):
    rank = a.shape[1]
    return call(
        sample_gram_kernel,
        "sample_gram",
        (1,),
        [whole(a.shape), whole(a.shape), NOWHERE],
        whole((rank, rank)),
        shaped(rank, rank),
        kept=kept,
    )(core, a, far, after)


def small_step_kernel(
    core_ref,
    a_ref,
    b_ref,
    gram_a_ref,
    gram_a_other_ref,
    gram_c_ref,
    gram_c_other_ref,
    drive_ref,
    drive_other_ref,
    drive_b_ref,
    drive_b_far_ref,
    after_ref,
    new_a_ref,
    new_b_ref,
    *refs,
):
    a, b = a_ref[...], b_ref[...]
    gram_a = gram_a_ref[...] + gram_a_other_ref[...]
    at_zero = core_ref[0] == 0
    mine, other = gram_c_ref[...], gram_c_other_ref[...]
    gram_c = jnp.concatenate([jnp.where(at_zero, mine, other), jnp.where(at_zero, other, mine)], 0)
    hessian_a = gram(b) * gram_c
    hessian_b = gram_a * gram_c
    drive_a = jnp.concatenate([drive_ref[...], drive_other_ref[...]], 0)
    drive_b = drive_b_ref[...] + drive_b_far_ref[...]
    new_a = a - (dot(a, hessian_a) - drive_a) * inverse_norm(hessian_a)
    new_b = b - (dot(b, hessian_b) - drive_b) * inverse_norm(hessian_b)
    new_a_ref[...] = new_a[: new_a_ref.shape[0]]
    new_b_ref[...] = new_b
    if refs:
        fill_khatri_rao(refs[0], new_a, new_b)


def small_step(core, a, b, args, after, kept, last):
    rows = a.shape[0] // 2 if last else a.shape[0]
    outs = [shaped(rows, a.shape[1]), shaped(*b.shape)]
    specs = [whole(outs[0].shape), whole(b.shape)]
    if not last:
        outs.append(pltpu.VMEM((2 * a.shape[1], a.shape[0] * b.shape[0]), BF16))
        specs.append(HELD)
    return call(
        small_step_kernel,
        "small_step",
        (1,),
        [whole(v.shape) for v in (a, b, *args)] + [NOWHERE],
        specs,
        outs,
        kept=kept,
    )(core, a, b, *args, after)


def swap(value, axis, size, distance):
    return lax.ppermute(value, axis, [(i, i ^ distance) for i in range(size)])


def local(mz, intensities, sample_start, scan_start, mass_start):
    b, c = scan_start, mass_start
    bins, rank = c.shape
    rows, scans = sample_start.shape[0], b.shape[0]
    x = intensities.reshape(-1, bins)
    number = lax.axis_index("grp") % 2
    core = number.reshape(1).astype(jnp.int32)

    def over_core(value):
        return swap(value, "grp", 4, 1)

    def over_x(value):
        return swap(value, "grp", 4, 2)

    def sum_mz(value, first, befores, kept, done=0):
        values = []
        distances = [1 << i for i in range(mz.bit_length() - 1)]
        place = distances.index(first)
        for distance in (distances[place:] + distances[:place])[: len(distances) - done]:
            far = swap(value, "mz", mz, distance)
            after, *befores = befores or [None]
            value = value + far if after is None else add(core, value, far, (after,), kept)
            values.append(value)
        return value, values[0]

    def close(keep, send, before, befores, kept):
        total = add(core, keep, over_core(send), before, kept)
        gram_c, _ = sum_mz(total[rows + scans :], mz // 2, [], kept)
        drive, early = sum_mz(total[: rows + scans], 1, befores, kept)
        drive, drive_b = drive[:rows], drive[rows:]
        return (gram_c, over_core(gram_c), drive, over_core(drive), drive_b, over_x(drive_b)), early

    def grams(a, far, after, kept):
        part = sample_gram(core, a[:rows], far, after, kept)
        return part, over_core(part)

    places = range(len(FIRST))
    others, after = [], x
    for place in places[:3]:
        after = give(core, x, after, place)
        others.append(over_core(after))
    a = jnp.concatenate([sample_start, over_core(sample_start)], 0)
    far_a = over_x(sample_start)

    near, *given = first_products(core, a, b, x, others[0], after, len(others))
    others += [over_core(value) for value in given]
    parts, nears = [], [near]
    kept = ()
    after = near
    krt, held = None, None
    for place in places:
        high, low, *rest = load(
            core, a, b, x, others[place], c, krt, held, after, kept, place, place == places[-1], FIRST[place]
        )
        if FIRST[place]:
            after, *rest = rest
            nears.append(after)
        if krt is None:
            krt = rest.pop()
        held = rest
        parts.append((high, low))
        kept += (high, low)
        if place == places[-1]:
            gram_a = grams(a, far_a, held[0], kept)
            c_mine = lax.dynamic_slice_in_dim(c, number * (bins // 2), bins // 2, 0)
            base, scale = mass_base(core, *gram_a, b, [c_mine], after, kept)

    fars = [over_x(near) for near in nears]
    news, sums = [], None
    kept_base = kept + (base,)

    def drives(place, after):
        nonlocal sums
        new, *sums = drive_products(
            core,
            a,
            b,
            scale,
            parts[place],
            base,
            nears[place],
            fars[place],
            sums,
            after,
            kept,
            place,
            place == places[-1],
        )
        news.append(new)
        return new

    old_a = a
    after = held[0]
    for place in places[len(nears) :]:
        after = mass_products(core, krt, parts[place], after, kept_base, 0, 2)
        nears.append(after)
        fars.append(over_x(nears[-1]))
    befores = [drives(0, nears[-1]), drives(1, nears[-1]), fars[2]]
    small, _ = close(*held, (fars[0], gram_a[0]), befores, kept_base)
    new_a, new_b, krt = small_step(core, a, b, (*gram_a, *small), news[-1], kept_base, False)

    a, b = new_a, new_b
    lasts, after = [], a
    for place, start, units in LAST:
        near = mass_products(core, krt, parts[place], after, kept_base, start, units)
        after = near
        if not lasts:
            far = over_x(jnp.concatenate([near, a[:rows]], 0))
            far, far_a = far[: units * UNIT], far[units * UNIT :]
        else:
            far = over_x(near)
        lasts.append((2 * place + start, near, far))
    for place in places[2:]:
        drives(place, after)
    total = add(core, sums[0], over_core(sums[1]), (news[-1],), ())
    drive, gram_c = total[: rows + scans], total[rows + scans :]
    drive = drive + swap(drive, "mz", mz, 1)
    gram_a = grams(a, far_a, drive, ())
    base, scale = mass_base(core, *gram_a, b, news, drive, ())
    stages = [[], [], []]
    for i in range(1, mz.bit_length() - 1):
        drive = drive + swap(drive, "mz", mz, 1 << i)
        stages[min(i, 2) - 1].append(drive)
    for i, distance in enumerate([mz >> 1] + [1 << i for i in range(mz.bit_length() - 2)]):
        gram_c = gram_c + swap(gram_c, "mz", mz, distance)
        stages[min(i, 2)].append(gram_c)
    drive, drive_b = drive[:rows], drive[rows:]
    small = gram_c, over_core(gram_c), drive, over_core(drive), drive_b, over_x(drive_b)
    stages[2] += small
    afters = [(scale,)] + stages
    mines = []
    out = None
    for place, (start, near, far) in enumerate(lasts):
        after = tuple(afters[place]) if place < len(afters) else ()
        if place > 1:
            after += (mark,)
        mine = last_step(core, scale, base, near, far, after, start)
        mines.append((mine, over_core(mine)))
        if place:
            out, mark = join(core, *mines[place - 1], out, mine, place - 1, bins)
    new_a, new_b = small_step(core, a, b, (*gram_a, *small), mines[-1][0], (), True)
    out, mark = join(core, *mines[-1], out, new_b, len(lasts) - 1, bins)
    return new_a, new_b, out


def solution(mesh):
    placed = (P("grp", None, "mz"), P("grp", None), P(), P("mz", None))
    return jax.shard_map(
        functools.partial(local, mesh.shape["mz"]),
        mesh=mesh,
        in_specs=placed,
        out_specs=(P("grp", None), P(), P("mz", None)),
        check_vma=False,
    )
```
